256 devices in a mesh: site: 64 (over z, x_hi, y), sp: 4 (over x_lo, core).
Axes of the slice: x: 4 (x_hi: 2, x_lo: 2; x = x_hi * 2 + x_lo), y: 4, z: 8, core: 2. Of those that a mesh axis runs over, the one named last changes fastest.
Arguments:
- counts: int32 [64, 5120, 2048], P('site', None, 'sp'), may hold values from 0 to 6
- factors: float32 [64, 16, 5120], P('site'), may hold values from -2.5 to 2.5
- loadings: float32 [2048, 16], P('sp'), may hold values from -0.4 to 0.4
- factor_momenta: float32 [64, 16, 5120], P('site'), may hold values from -6 to 6
- loading_momenta: float32 [2048, 16], P('sp'), may hold values from -6 to 6
- precision: float32 [16], replicated, may hold values from 0.5 to 4
- factor_step: float32 [1], replicated, may hold values from 0.03 to 0.07
- loading_step: float32 [1], replicated, may hold values from 0.0002 to 0.0008
Outputs:
- new_factors: float32 [64, 16, 5120], P('site')
- new_factor_momenta: float32 [64, 16, 5120], P('site')
- new_loadings: float32 [2048, 16], P('sp')
- new_loading_momenta: float32 [2048, 16], P('sp')
- energy: float32 [1], replicated
The draws below stay inside these ranges and needn't reach their ends.
All inputs are finite; a program needn't handle non-finite values.
Results may differ from the reference program's by a relative error of at most 0.0001.
Values sent between devices are 32-bit elements; how exact they have to be, the bound alone decides.
A program may use at most 128 MiB of HBM per device.

```python
import math
import jax
import jax.numpy as jnp
from jax import lax

K = 16
TX = 80
TY = 64
TGY = 8
TGX = 8
CELLS = 5120
GX = 640
GY = 512
SPECIES = 2048
N_SITE = 64


def plant(drawn, rng, smallest, top_value):
    spot = [jax.random.randint(jax.random.fold_in(rng, axis), (), 0, length) for axis, length in enumerate(drawn.shape)]
    widest = drawn.shape.index(max(drawn.shape))
    beside = spot[:widest] + [(spot[widest] + 1) % drawn.shape[widest]] + spot[widest + 1:]
    return drawn.at[tuple(spot)].set(smallest).at[tuple(beside)].set(top_value)


def steps_of(key, dims, split, smallest, high):
    factor_of = 1.0
    for position, parts in split:
        steps = jax.random.uniform(jax.random.fold_in(jax.random.fold_in(key, 6), position), (parts,), jnp.float32, smallest / len(split), high / len(split))
        factor_of = factor_of * jnp.repeat(jnp.exp(steps), dims[position] // parts).reshape((-1,) + (1,) * (len(dims) - 1 - position))
    return factor_of


def centred(own_key, dims, spread, limit, cuts=(), dtype=jnp.bfloat16):
    entries = jax.random.normal(own_key, dims, jnp.float32) * spread
    if len(cuts) > 0:
        entries = steps_of(own_key, dims, cuts, -0.22, 0.18) * entries
    return jnp.clip(entries, min=-limit, max=limit).astype(dtype)


def setup_inputs(seed: int = 0) -> dict:
    arg_keys = jax.random.split(jax.random.key(seed), 9)
    return {
        "counts": plant(jax.random.randint(arg_keys[0], (N_SITE, CELLS, SPECIES), 0, 7), jax.random.fold_in(arg_keys[0], 1), 0, 6).astype(jnp.int32),
        "factors": centred(arg_keys[1], (N_SITE, K, CELLS), 1.0, 2.5, ((0, 64),), jnp.float32),
        "loadings": centred(arg_keys[2], (SPECIES, K), 0.15, 0.4, ((0, 4),), jnp.float32),
        "factor_momenta": centred(arg_keys[3], (N_SITE, K, CELLS), 1.0, 6.0, ((0, 64),), jnp.float32),
        "loading_momenta": centred(arg_keys[4], (SPECIES, K), 1.0, 6.0, ((0, 4),), jnp.float32),
        "precision": jnp.clip(jnp.exp(jax.random.uniform(arg_keys[5], (K,), jnp.float32, math.log(0.5), math.log(4.0))), 0.5, 4.0),
        "factor_step": jnp.clip(jax.random.uniform(arg_keys[6], (1,), jnp.float32, 0.03, 0.07), 0.03, 0.07),
        "loading_step": jnp.clip(jnp.exp(jax.random.uniform(arg_keys[7], (1,), jnp.float32, math.log(0.0002), math.log(0.0008))), 0.0002, 0.0008),
    }


kappa_sq = 0.25
highest = lax.Precision.HIGHEST


def to_grid(tiles):
    shaped = tiles.reshape(TGX, TGY, K, TX, TY)
    return shaped.transpose(2, 0, 3, 1, 4).reshape(K, TGX * TX, TGY * TY)


def from_grid(whole):
    shaped = whole.reshape(K, TGX, TX, TGY, TY)
    return shaped.transpose(1, 3, 0, 2, 4).reshape(N_SITE, K, TX * TY)


def to_strip(tiles):
    shaped = tiles.reshape(TGX, TGY, K, TX, TY)
    return shaped.transpose(2, 3, 0, 1, 4).reshape(K, TX, TGX * TGY * TY)


def from_strip(strip):
    shaped = strip.reshape(K, TX, TGX, TGY, TY)
    return shaped.transpose(2, 3, 0, 1, 4).reshape(N_SITE, K, TX * TY)


def apply_prior(tiles):
    whole = to_grid(tiles)
    padded = jnp.pad(whole, ((0, 0), (1, 1), (0, 0)))
    vertical = padded[:, 2:, :] + padded[:, :-2, :]
    strip = to_strip(tiles)
    padded_strip = jnp.pad(strip, ((0, 0), (0, 0), (1, 1)))
    horizontal = padded_strip[:, :, 2:] + padded_strip[:, :, :-2]
    beside = from_grid(vertical) + from_strip(horizontal)
    return (kappa_sq + 4.0) * tiles - beside


def poisson_terms(factors, loadings, counts):
    def one_tile(carry, tile_pair):
        tile, tile_counts = tile_pair
        counts_f = tile_counts.astype(jnp.float32)
        log_rate = lax.dot_general(tile, loadings, (((0,), (1,)), ((), ())), precision=highest, preferred_element_type=jnp.float32)
        intensity = jnp.exp(log_rate)
        residual = counts_f - intensity
        factor_part = lax.dot_general(loadings, residual, (((0,), (1,)), ((), ())), precision=highest, preferred_element_type=jnp.float32)
        loading_part = lax.dot_general(residual, tile, (((0,), (1,)), ((), ())), precision=highest, preferred_element_type=jnp.float32)
        loglik = jnp.sum(counts_f * log_rate - intensity)
        return (carry[0] + loading_part, carry[1] + loglik), factor_part

    start = (jnp.zeros((SPECIES, K), jnp.float32), jnp.zeros((), jnp.float32))
    (loading_part, loglik), factor_part = lax.scan(one_tile, start, (factors, counts))
    return factor_part, loading_part, loglik


def gradient(factors, loadings, counts, precision):
    factor_part, loading_part, loglik = poisson_terms(factors, loadings, counts)
    prior = apply_prior(factors)
    factor_grad = factor_part - precision[None, :, None] * prior
    loading_grad = loading_part - loadings
    return factor_grad, loading_grad, loglik, prior


def reference(counts, factors, loadings, factor_momenta, loading_momenta, precision, factor_step, loading_step):
    step_factor = factor_step[0]
    step_loading = loading_step[0]
    factor_grad, loading_grad, _, _ = gradient(factors, loadings, counts, precision)
    half_factor = factor_momenta + 0.5 * step_factor * factor_grad
    half_loading = loading_momenta + 0.5 * step_loading * loading_grad
    new_factors = factors + step_factor * half_factor
    new_loadings = loadings + step_loading * half_loading
    factor_grad, loading_grad, loglik, prior = gradient(new_factors, new_loadings, counts, precision)
    end_factor = half_factor + 0.5 * step_factor * factor_grad
    end_loading = half_loading + 0.5 * step_loading * loading_grad
    potential = -loglik + 0.5 * jnp.sum(precision[None, :, None] * new_factors * prior) + 0.5 * jnp.sum(new_loadings * new_loadings)
    kinetic = 0.5 * jnp.sum(end_factor * end_factor) + 0.5 * jnp.sum(end_loading * end_loading)
    energy = jnp.reshape((potential + kinetic) / (GX * GY * SPECIES), (1,))
    return new_factors, end_factor, new_loadings, end_loading, energy
```

```python
import math

import jax
import jax.numpy as jnp
from jax import lax
from jax.experimental import pallas as pl
from jax.experimental.pallas import tpu as pltpu
from jax.sharding import Mesh
from jax.sharding import PartitionSpec as P

SITE = ("z", "xh", "y")
SP = ("xl", "core")
K = 16
TY = 64
CELLS = 5120
SPEC = 512
NZ = 8
NG = 8
TOTAL = 640 * 512 * 2048
S = 512
NS = CELLS // S
W = 1024
NW = CELLS // W
H = W // 2
NB = CELLS // 128
PAD = CELLS + 256
LOG2E = math.log2(math.e)
LN2 = math.log(2.0)
f32 = jnp.float32
bf16 = jnp.bfloat16
NT = (((1,), (1,)), ((), ()))
TN = (((0,), (0,)), ((), ()))


def split(value):
    high = value.astype(bf16)
    low = (value - high.astype(f32)).astype(bf16)
    return high, low


def lanes(shape=(K, 128)):
    return lax.broadcasted_iota(jnp.int32, shape, 1)


def kernel(
    counts_hbm, fac_hbm, ld_hbm, fmom_hbm, lmom_hbm, prec_ref, fstep_ref, lstep_ref,
    nf_hbm, nfm_hbm, nl_hbm, nlm_hbm, en_ref,
    cv, fv, lv, fm, lm, zp, cols, halo, zt, ls, lt, rh, rl, lacc, tacc,
    fs, crecv, xs, xrecv, gs, base, half, efac, nl, hl, elo,
    sb1, rb1, sb2, rb2, sb3, rb3, es, er, ct,
    csem, isem, osem, hsend, hrecv, asend, arecv, fsend, frecv, esend, erecv,
):
    z = lax.axis_index("z")
    xh = lax.axis_index("xh")
    y = lax.axis_index("y")
    xl = lax.axis_index("xl")
    core = lax.axis_index("core")
    g = xh * 4 + y
    site = z * NG + g

    def at_g(i):
        return {"xh": i // 4, "y": i % 4}

    def at_site(i):
        return {"z": i // NG, "xh": (i % NG) // 4, "y": i % 4}

    other_core = {"core": 1 - core}
    other_chip = {"xl": 1 - xl}
    other_both = {"xl": 1 - xl, "core": 1 - core}
    has_up, has_down = z > 0, z < NZ - 1
    has_left, has_right = site > 0, site < NZ * NG - 1
    carry_left = jnp.logical_and(g == 0, has_left)
    carry_right = jnp.logical_and(g == NG - 1, has_right)

    ins = [
        pltpu.make_async_copy(src, dst, isem.at[i])
        for i, (src, dst) in enumerate(
            ((fac_hbm, fv), (ld_hbm, lv), (fmom_hbm, fm), (lmom_hbm, lm))
        )
    ]

    def counts_in(i):
        rows = pl.ds(pl.multiple_of(i * S, S), S)
        return pltpu.make_async_copy(counts_hbm.at[rows], cv.at[rows], csem.at[i])

    ins[0].start()
    ins[1].start()
    for i in range(NS):
        counts_in(i).start()
    ins[2].start()
    ins[3].start()

    barrier = pltpu.get_barrier_semaphore()

    def greet(device):
        pl.semaphore_signal(barrier, inc=1, device_id=device, device_id_type=pl.DeviceIdType.MESH)

    for device in (other_core, other_chip, other_both):
        greet(device)
    for d in range(1, NZ):
        greet({"z": (z + d) % NZ})
    for d in range(1, NG):
        greet(at_g((g + d) % NG))

    @pl.when(carry_left)
    def _():
        greet(at_site(site - 1))

    @pl.when(carry_right)
    def _():
        greet(at_site(site + 1))

    zeros = jnp.zeros((K, 128), f32)
    for r in range(2):

        @pl.when(jnp.logical_not(has_up))
        def _():
            zp[r, :, pl.ds(0, 128)] = zeros

        @pl.when(jnp.logical_not(has_down))
        def _():
            zp[r, :, pl.ds(PAD - 128, 128)] = zeros

        @pl.when(jnp.logical_not(has_left))
        def _():
            halo[r, 0] = zeros

        @pl.when(jnp.logical_not(has_right))
        def _():
            halo[r, 1] = zeros

    def remote(src, dst, send, recv, device):
        return pltpu.make_async_remote_copy(
            src_ref=src, dst_ref=dst, send_sem=send, recv_sem=recv,
            device_id=device, device_id_type=pl.DeviceIdType.MESH,
        )

    def pack_columns(r):
        def body(j, both):
            first, last = both
            block = zp[r, :, pl.ds(pl.multiple_of(128 + j * 128, 128), 128)]
            here = lanes() % TY == j
            first = jnp.where(here, pltpu.roll(block, j, 1), first)
            last = jnp.where(here, pltpu.roll(block, j + 65, 1), last)
            return first, last

        first, last = lax.fori_loop(0, NB, body, (zeros, zeros))
        cols[r, 0] = first
        cols[r, 1] = last

    def rim_copies(r):
        return (
            (
                has_down,
                has_up,
                remote(zp.at[r, :, pl.ds(PAD - 256, 128)], zp.at[r, :, pl.ds(0, 128)],
                       hsend.at[r, 0], hrecv.at[r, 0], {"z": lax.min(z + 1, NZ - 1)}),
            ),
            (
                has_up,
                has_down,
                remote(zp.at[r, :, pl.ds(128, 128)], zp.at[r, :, pl.ds(PAD - 128, 128)],
                       hsend.at[r, 1], hrecv.at[r, 1], {"z": lax.max(z - 1, 0)}),
            ),
            (
                has_right,
                has_left,
                remote(cols.at[r, 1], halo.at[r, 0], hsend.at[r, 2], hrecv.at[r, 2],
                       at_site(lax.min(site + 1, NZ * NG - 1))),
            ),
            (
                has_left,
                has_right,
                remote(cols.at[r, 0], halo.at[r, 1], hsend.at[r, 3], hrecv.at[r, 3],
                       at_site(lax.max(site - 1, 0))),
            ),
        )

    def send_rims(r):
        for sends, _, copy in rim_copies(r):
            pl.when(sends)(copy.start)

    def wait_rims(r):
        for sends, receives, copy in rim_copies(r):
            pl.when(sends)(copy.wait_send)
            pl.when(receives)(copy.wait_recv)

    def prior_block(r, j):
        def block_at(i):
            return zp[r, :, pl.ds(pl.multiple_of(i * 128, 128), 128)]

        before, block, after = block_at(j), block_at(j + 1), block_at(j + 2)
        lane = lanes()
        low = lane < TY
        up = pltpu.roll(jnp.where(low, block, before), TY, 1)
        down = pltpu.roll(jnp.where(low, after, block), TY, 1)
        left = jnp.where(
            lane % TY == 0, pltpu.roll(halo[r, 0], (128 - j) % 128, 1), pltpu.roll(block, 1, 1)
        )
        right = jnp.where(
            lane % TY == TY - 1, pltpu.roll(halo[r, 1], TY - 1 - j, 1), pltpu.roll(block, 127, 1)
        )
        return block, 4.25 * block - (up + down + left + right)

    def split_factors(r):
        high, low = split(zp[r, :, pl.ds(128, CELLS)])
        zt[0:16] = high
        zt[16:32] = low
        zt[32:48] = high

    def split_loadings(value):
        high, low = split(value * LOG2E)
        ls[0:16] = high
        ls[16:32] = high
        ls[32:48] = low
        high, low = split(value)
        lt[0:16] = high
        lt[16:32] = low

    def residual_step(i, r):
        rows = pl.ds(pl.multiple_of(i * S, S), S)
        log2_rate = lax.dot_general(zt[:, rows], ls[...], TN, preferred_element_type=f32)
        intensity = jnp.exp2(log2_rate)
        count = cv[rows, :].astype(f32)
        high, low = split(count - intensity)
        rh[rows, :] = high
        rl[rows, :] = low
        lacc[0:32] += jnp.dot(zt[0:32, rows], high, preferred_element_type=f32)
        lacc[32:48] += jnp.dot(zt[0:16, rows], low, preferred_element_type=f32)
        if r == 1:
            tacc[0] += jnp.sum((count * log2_rate).reshape(S // 8, 8, SPEC), axis=0)
            tacc[1] += jnp.sum(intensity.reshape(S // 8, 8, SPEC), axis=0)

    def factor_step_part(i):
        rows = slice(i * W, (i + 1) * W)
        a = lax.dot_general(lt[0:32], rh[rows, :], NT, preferred_element_type=f32)
        b = lax.dot_general(lt[0:16], rl[rows, :], NT, preferred_element_type=f32)
        fs[:, rows] = a[0:16] + a[16:32] + b

    def tiles_of(value):
        return [value[8 * (p // 4) : 8 * (p // 4) + 8, 128 * (p % 4) : 128 * (p % 4) + 128]
                for p in range(NZ)]

    def spread(r, phase, source, target, me, count, where):
        def copy(d):
            to = (me + d) % count
            return remote(source(to), target.at[r, me], asend.at[r, phase, d],
                          arecv.at[r, phase, me], where(to))

        def arrival(d):
            of = (me + d) % count
            return remote(source(of), target.at[r, of], asend.at[r, phase, d],
                          arecv.at[r, phase, of], where(of))

        def start():
            for d in range(1, count):
                copy(d).start()

        def wait():
            for d in range(1, count):
                arrival(d).wait_recv()

        def sent():
            for d in range(1, count):
                copy(d).wait_send()

        return start, wait, sent

    def at_z(i):
        return {"z": i}

    def phases(r):
        return (
            spread(r, 0, lambda to: sb1.at[r, to], rb1, z, NZ, at_z),
            spread(r, 1, lambda to: sb2.at[r], rb2, g, NG, at_g),
            spread(r, 2, lambda to: sb3.at[r], rb3, z, NZ, at_z),
        )

    def sum_begin(r):
        part = lacc[0:16] + lacc[16:32] + lacc[32:48]
        for p, tile in enumerate(tiles_of(part)):
            sb1[r, p] = tile
        phases(r)[0][0]()
        rb1[r, z] = sb1[r, z]

    def added(ref, r):
        v = [ref[r, p] for p in range(8)]
        return ((v[0] + v[1]) + (v[2] + v[3])) + ((v[4] + v[5]) + (v[6] + v[7]))

    def sum_second(r):
        phases(r)[0][1]()
        value = added(rb1, r)
        sb2[r] = value
        phases(r)[1][0]()
        rb2[r, g] = value

    def sum_third(r):
        phases(r)[1][1]()
        value = added(rb2, r)
        sb3[r] = value
        phases(r)[2][0]()
        rb3[r, z] = value

    def sum_end(r):
        phases(r)[2][1]()
        for phase in phases(r):
            phase[2]()
        v = [rb3[r, p] for p in range(NZ)]
        return jnp.concatenate(
            [jnp.concatenate(v[0:4], axis=1), jnp.concatenate(v[4:8], axis=1)], axis=0
        )

    def mine(i, who):
        return pl.ds(pl.multiple_of(i * W + who * H, H), H)

    def core_copy(r, i):
        return remote(fs.at[:, mine(i, 1 - core)], crecv.at[r, i],
                      fsend.at[r, 0, i], frecv.at[r, 0, i], other_core)

    def chip_copy(r, i):
        return remote(xs.at[i], xrecv.at[r, i],
                      fsend.at[r, 1, i], frecv.at[r, 1, i], other_chip)

    def back_copy(r, i):
        where = gs.at[r, :, mine(i, core)]
        return remote(where, where, fsend.at[r, 2, i], frecv.at[r, 2, i], other_core)

    def chip_sum(r, i):
        core_copy(r, i).wait_recv()
        xs[i] = fs[:, mine(i, core)] + crecv[r, i]
        chip_copy(r, i).start()

    def full_sum(r, i):
        chip_copy(r, i).wait_recv()
        gs[r, :, mine(i, core)] = xs[i] + xrecv[r, i]
        back_copy(r, i).start()

    def back_wait(r, i):
        remote(gs.at[r, :, mine(i, core)], gs.at[r, :, mine(i, 1 - core)],
               fsend.at[r, 2, i], frecv.at[r, 2, i], other_core).wait_recv()

    def exchange(r, between):
        for i in range(NW + 2):
            if i < NW:
                factor_step_part(i)
                core_copy(r, i).start()
            if 1 <= i < NW + 1:
                chip_sum(r, i - 1)
            if 2 <= i:
                full_sum(r, i - 2)
            between(i)
        for i in range(NW):
            back_wait(r, i)
            core_copy(r, i).wait_send()
            chip_copy(r, i).wait_send()
            back_copy(r, i).wait_send()

    step_f = fstep_ref[0]
    step_l = lstep_ref[0]
    row = lax.broadcasted_iota(jnp.int32, (K, 128), 0)
    gain = zeros
    for k in range(K):
        gain = jnp.where(row == k, prec_ref[k], gain)

    ins[0].wait()
    zp[0, :, pl.ds(128, CELLS)] = fv[...]
    split_factors(0)
    ins[1].wait()
    split_loadings(lv[...])
    lacc[...] = jnp.zeros_like(lacc)
    tacc[...] = jnp.zeros_like(tacc)
    pack_columns(0)

    def first_loop(i, carry):
        counts_in(i).wait()
        residual_step(i, 0)
        return carry

    lax.fori_loop(0, NS, first_loop, 0)

    pl.semaphore_wait(
        barrier, 17 + carry_left.astype(jnp.int32) + carry_right.astype(jnp.int32)
    )
    sum_begin(0)
    send_rims(0)

    def prior_first():
        wait_rims(0)
        ins[2].wait()

        def body(j, carry):
            here = pl.ds(pl.multiple_of(j * 128, 128), 128)
            _, prior = prior_block(0, j)
            base[:, here] = fm[:, here] - (0.5 * step_f) * (gain * prior)
            return carry

        lax.fori_loop(0, NB, body, 0)

    def between_first(i):
        if i == 2:
            sum_second(0)
        if i == 3:
            prior_first()
        if i == 5:
            sum_third(0)

    exchange(0, between_first)

    half_now = base[...] + (0.5 * step_f) * gs[0]
    half[...] = half_now
    zp[1, :, pl.ds(128, CELLS)] = fv[...] + step_f * half_now
    split_factors(1)
    pack_columns(1)
    send_rims(1)
    nf_out = pltpu.make_async_copy(zp.at[1, :, pl.ds(128, CELLS)], nf_hbm, osem.at[0])
    nf_out.start()

    grad_l = sum_end(0) - lv[...]
    ins[3].wait()
    half_l = lm[...] + (0.5 * step_l) * grad_l
    hl[...] = half_l
    nl[...] = lv[...] + step_l * half_l
    split_loadings(nl[...])
    nl_out = pltpu.make_async_copy(nl, nl_hbm, osem.at[1])
    nl_out.start()

    lacc[...] = jnp.zeros_like(lacc)

    def second_loop(i, carry):
        residual_step(i, 1)
        return carry

    lax.fori_loop(0, NS, second_loop, 0)
    sum_begin(1)

    def prior_second():
        wait_rims(1)

        def body(j, total):
            here = pl.ds(pl.multiple_of(j * 128, 128), 128)
            block, prior = prior_block(1, j)
            weighted = gain * prior
            base[:, here] = half[:, here] - (0.5 * step_f) * weighted
            return total + block * weighted

        ct[0] = lax.fori_loop(0, NB, body, zeros)

    def between_second(i):
        if i == 2:
            sum_second(1)
        if i == 3:
            prior_second()
        if i == 5:
            sum_third(1)

    exchange(1, between_second)

    end_f = base[...] + (0.5 * step_f) * gs[1]
    efac[...] = end_f
    nfm_out = pltpu.make_async_copy(efac, nfm_hbm, osem.at[2])
    nfm_out.start()

    local = jnp.sum(tacc[1] - LN2 * tacc[0]) + 0.125 * (
        jnp.sum(ct[0]) + jnp.sum(end_f * end_f)
    )

    grad_l = sum_end(1) - nl[...]
    end_l = hl[...] + (0.5 * step_l) * grad_l
    elo[...] = end_l
    nlm_out = pltpu.make_async_copy(elo, nlm_hbm, osem.at[3])
    nlm_out.start()

    def scalar_sum(phase, value, me, where):
        es[phase] = jnp.full((8, 128), value, f32)

        def copy(d):
            to = (me + d) % 8
            return remote(es.at[phase], er.at[phase, me], esend.at[phase, d],
                          erecv.at[phase, me], where(to))

        def arrival(d):
            of = (me + d) % 8
            return remote(es.at[phase], er.at[phase, of], esend.at[phase, d],
                          erecv.at[phase, of], where(of))

        for d in range(1, 8):
            copy(d).start()
        er[phase, me] = es[phase]
        for d in range(1, 8):
            arrival(d).wait_recv()
        for d in range(1, 8):
            copy(d).wait_send()
        return added(er, phase)

    total = scalar_sum(0, local, g, at_g)[0, 0]
    total = scalar_sum(1, total, z, at_z)[0, 0]
    total = total + 0.5 * (jnp.sum(nl[...] * nl[...]) + jnp.sum(end_l * end_l))
    es[2] = jnp.full((8, 128), total, f32)
    me = xl * 2 + core
    sp = (
        (other_core, xl * 2 + (1 - core)),
        (other_chip, (1 - xl) * 2 + core),
        (other_both, (1 - xl) * 2 + (1 - core)),
    )
    for d, (device, _) in enumerate(sp):
        remote(es.at[2], er.at[2, me], esend.at[2, d], erecv.at[2, me], device).start()
    er[2, me] = es[2]
    for d, (device, slot) in enumerate(sp):
        remote(es.at[2], er.at[2, slot], esend.at[2, d], erecv.at[2, slot], device).wait_recv()
    for d, (device, _) in enumerate(sp):
        remote(es.at[2], er.at[2, me], esend.at[2, d], erecv.at[2, me], device).wait_send()
    total = (er[2, 0] + er[2, 1]) + (er[2, 2] + er[2, 3])
    en_ref[0] = (total / TOTAL)[0, 0]
    for copy in (nf_out, nl_out, nfm_out, nlm_out):
        copy.wait()


def local(
    counts, factors, loadings, factor_momenta, loading_momenta, precision, factor_step, loading_step
):
    hbm = pl.BlockSpec(memory_space=pl.ANY)
    smem = pl.BlockSpec(memory_space=pltpu.SMEM)
    vm = pltpu.VMEM
    dma = pltpu.SemaphoreType.DMA
    outs = pl.pallas_call(
        kernel,
        out_shape=(
            jax.ShapeDtypeStruct((K, CELLS), f32),
            jax.ShapeDtypeStruct((K, CELLS), f32),
            jax.ShapeDtypeStruct((K, SPEC), f32),
            jax.ShapeDtypeStruct((K, SPEC), f32),
            jax.ShapeDtypeStruct((1,), f32),
        ),
        in_specs=[hbm] * 5 + [smem] * 3,
        out_specs=(hbm, hbm, hbm, hbm, smem),
        scratch_shapes=[
            vm((CELLS, SPEC), jnp.int32),
            vm((K, CELLS), f32),
            vm((K, SPEC), f32),
            vm((K, CELLS), f32),
            vm((K, SPEC), f32),
            vm((2, K, PAD), f32),
            vm((2, 2, K, 128), f32),
            vm((2, 2, K, 128), f32),
            vm((48, CELLS), bf16),
            vm((48, SPEC), bf16),
            vm((32, SPEC), bf16),
            vm((CELLS, SPEC), bf16),
            vm((CELLS, SPEC), bf16),
            vm((48, SPEC), f32),
            vm((2, 8, SPEC), f32),
            vm((K, CELLS), f32),
            vm((2, NW, K, H), f32),
            vm((NW, K, H), f32),
            vm((2, NW, K, H), f32),
            vm((2, K, CELLS), f32),
            vm((K, CELLS), f32),
            vm((K, CELLS), f32),
            vm((K, CELLS), f32),
            vm((K, SPEC), f32),
            vm((K, SPEC), f32),
            vm((K, SPEC), f32),
            vm((2, 8, 8, 128), f32),
            vm((2, 8, 8, 128), f32),
            vm((2, 8, 128), f32),
            vm((2, 8, 8, 128), f32),
            vm((2, 8, 128), f32),
            vm((2, 8, 8, 128), f32),
            vm((3, 8, 128), f32),
            vm((3, 8, 8, 128), f32),
            vm((1, K, 128), f32),
            dma((NS,)),
            dma((4,)),
            dma((4,)),
            dma((2, 4)),
            dma((2, 4)),
            dma((2, 3, 8)),
            dma((2, 3, 8)),
            dma((2, 3, NW)),
            dma((2, 3, NW)),
            dma((3, 8)),
            dma((3, 8)),
        ],
        compiler_params=pltpu.CompilerParams(
            collective_id=0, has_side_effects=True, vmem_limit_bytes=56 * 1024 * 1024
        ),
        name="leapfrog",
    )(
        counts[0], factors[0], loadings.T, factor_momenta[0], loading_momenta.T,
        precision, factor_step, loading_step,
    )
    new_factors, end_factor, new_loadings, end_loading, energy = outs
    return new_factors[None], end_factor[None], new_loadings.T, end_loading.T, energy


def solution(mesh):
    torus = Mesh(mesh.devices.reshape(8, 2, 4, 2, 2), SITE + SP)
    placed = (
        P(SITE, None, SP),
        P(SITE, None, None),
        P(SP, None),
        P(SITE, None, None),
        P(SP, None),
        P(),
        P(),
        P(),
    )
    return jax.shard_map(
        local,
        mesh=torus,
        in_specs=placed,
        out_specs=(P(SITE, None, None), P(SITE, None, None), P(SP, None), P(SP, None), P()),
        check_vma=False,
    )
```

```python
import math

import jax
import jax.numpy as jnp
from jax import lax
from jax.experimental import pallas as pl
from jax.experimental.pallas import tpu as pltpu
from jax.sharding import Mesh
from jax.sharding import PartitionSpec as P

SITE = ("z", "xh", "y")
SP = ("xl", "core")
K = 16
TY = 64
CELLS = 5120
SPEC = 512
NZ = 8
NG = 8
TOTAL = 640 * 512 * 2048
S = 1280
NS = CELLS // S
SH = SPEC // 2
W = 1024
NW = CELLS // W
H = W // 2
NB = CELLS // 128
PAD = CELLS + 256
LOG2E = math.log2(math.e)
LN2 = math.log(2.0)
f32 = jnp.float32
bf16 = jnp.bfloat16
NT = (((1,), (1,)), ((), ()))
TN = (((0,), (0,)), ((), ()))


def split(value):
    high = value.astype(bf16)
    low = (value - high.astype(f32)).astype(bf16)
    return high, low


def lanes(shape=(K, 128)):
    return lax.broadcasted_iota(jnp.int32, shape, 1)


def kernel(
    counts_hbm, fac_hbm, ld_hbm, fmom_hbm, lmom_hbm, prec_hbm, fstep_hbm, lstep_hbm,
    nf_hbm, nfm_hbm, nl_hbm, nlm_hbm, en_ref,
    prec_ref, fstep_ref, lstep_ref,
    cv, fv, lv, fm, lm, zp, cols, halo, zt, zs, ls, lt, rh, rl, lacc, tacc,
    fs, crecv, xs, xrecv, gs, base, half, efac, nl, hl, elo, ct,
    sa, ra, sb, rb, es, er,
    csem, isem, osem, hsend, hrecv, asend, arecv, fsend, frecv, esend, erecv,
):
    z = lax.axis_index("z")
    xh = lax.axis_index("xh")
    y = lax.axis_index("y")
    xl = lax.axis_index("xl")
    core = lax.axis_index("core")
    g = xh * 4 + y
    site = z * NG + g

    def at_g(i):
        return {"xh": i // 4, "y": i % 4}

    def at_site(i):
        return {"z": i // NG, "xh": (i % NG) // 4, "y": i % 4}

    other_core = {"core": 1 - core}
    other_chip = {"xl": 1 - xl}
    other_both = {"xl": 1 - xl, "core": 1 - core}
    has_up, has_down = z > 0, z < NZ - 1
    has_left, has_right = site > 0, site < NZ * NG - 1
    carry_left = jnp.logical_and(g == 0, has_left)
    carry_right = jnp.logical_and(g == NG - 1, has_right)

    ins = [
        pltpu.make_async_copy(src, dst, isem.at[i])
        for i, (src, dst) in enumerate(
            (
                (fac_hbm, fv), (ld_hbm, lv), (fmom_hbm, fm), (lmom_hbm, lm),
                (prec_hbm, prec_ref), (fstep_hbm, fstep_ref), (lstep_hbm, lstep_ref),
            )
        )
    ]

    def counts_in(h, i):
        rows, columns = slice(i * S, (i + 1) * S), slice(h * SH, (h + 1) * SH)
        return pltpu.make_async_copy(
            counts_hbm.at[rows, columns], cv.at[rows, columns], csem.at[h, i]
        )

    ins[0].start()
    ins[1].start()
    for h in range(2):
        for i in range(NS):
            counts_in(h, i).start()
    for copy in ins[2:]:
        copy.start()

    barrier = pltpu.get_barrier_semaphore()

    def greet(device):
        pl.semaphore_signal(barrier, inc=1, device_id=device, device_id_type=pl.DeviceIdType.MESH)

    for device in (other_core, other_chip, other_both):
        greet(device)
    for d in range(1, NZ):
        greet({"z": (z + d) % NZ})
    for d in range(1, NG):
        greet(at_g((g + d) % NG))

    @pl.when(carry_left)
    def _():
        greet(at_site(site - 1))

    @pl.when(carry_right)
    def _():
        greet(at_site(site + 1))

    zeros = jnp.zeros((K, 128), f32)
    for r in range(2):

        @pl.when(jnp.logical_not(has_up))
        def _():
            zp[r, :, pl.ds(0, 128)] = zeros

        @pl.when(jnp.logical_not(has_down))
        def _():
            zp[r, :, pl.ds(PAD - 128, 128)] = zeros

        @pl.when(jnp.logical_not(has_left))
        def _():
            halo[r, 0] = zeros

        @pl.when(jnp.logical_not(has_right))
        def _():
            halo[r, 1] = zeros

    def remote(src, dst, send, recv, device):
        return pltpu.make_async_remote_copy(
            src_ref=src, dst_ref=dst, send_sem=send, recv_sem=recv,
            device_id=device, device_id_type=pl.DeviceIdType.MESH,
        )

    def pack_columns(r):
        def body(j, both):
            first, last = both
            block = zp[r, :, pl.ds(pl.multiple_of(128 + j * 128, 128), 128)]
            here = lanes() % TY == j
            first = jnp.where(here, pltpu.roll(block, j, 1), first)
            last = jnp.where(here, pltpu.roll(block, j + 65, 1), last)
            return first, last

        first, last = lax.fori_loop(0, NB, body, (zeros, zeros), unroll=8)
        cols[r, 0] = first
        cols[r, 1] = last

    def rim_copies(r):
        return (
            (
                has_down,
                has_up,
                remote(zp.at[r, :, pl.ds(PAD - 256, 128)], zp.at[r, :, pl.ds(0, 128)],
                       hsend.at[r, 0], hrecv.at[r, 0], {"z": lax.min(z + 1, NZ - 1)}),
            ),
            (
                has_up,
                has_down,
                remote(zp.at[r, :, pl.ds(128, 128)], zp.at[r, :, pl.ds(PAD - 128, 128)],
                       hsend.at[r, 1], hrecv.at[r, 1], {"z": lax.max(z - 1, 0)}),
            ),
            (
                has_right,
                has_left,
                remote(cols.at[r, 1], halo.at[r, 0], hsend.at[r, 2], hrecv.at[r, 2],
                       at_site(lax.min(site + 1, NZ * NG - 1))),
            ),
            (
                has_left,
                has_right,
                remote(cols.at[r, 0], halo.at[r, 1], hsend.at[r, 3], hrecv.at[r, 3],
                       at_site(lax.max(site - 1, 0))),
            ),
        )

    def send_rims(r):
        for sends, _, copy in rim_copies(r):
            pl.when(sends)(copy.start)

    def wait_rims(r):
        for sends, receives, copy in rim_copies(r):
            pl.when(sends)(copy.wait_send)
            pl.when(receives)(copy.wait_recv)

    def prior_block(r, j):
        def block_at(i):
            return zp[r, :, pl.ds(pl.multiple_of(i * 128, 128), 128)]

        before, block, after = block_at(j), block_at(j + 1), block_at(j + 2)
        lane = lanes()
        low = lane < TY
        up = pltpu.roll(jnp.where(low, block, before), TY, 1)
        down = pltpu.roll(jnp.where(low, after, block), TY, 1)
        left = jnp.where(
            lane % TY == 0, pltpu.roll(halo[r, 0], (128 - j) % 128, 1), pltpu.roll(block, 1, 1)
        )
        right = jnp.where(
            lane % TY == TY - 1, pltpu.roll(halo[r, 1], TY - 1 - j, 1), pltpu.roll(block, 127, 1)
        )
        return block, 4.25 * block - (up + down + left + right)

    def split_factors(value, rows):
        high, low = split(value)
        both = jnp.concatenate([high, low, high], axis=0)
        zt[:, rows] = both
        zs[rows, :] = both.T

    def split_loadings(value, h):
        columns = slice(h * SH, (h + 1) * SH)
        high, low = split(value * LOG2E)
        ls[0:16, columns] = high
        ls[16:32, columns] = high
        ls[32:48, columns] = low
        high, low = split(value)
        lt[0:16, columns] = high
        lt[16:32, columns] = low

    def residual_pass(r, h):
        columns = slice(h * SH, (h + 1) * SH)
        for i in range(NS):
            rows = slice(i * S, (i + 1) * S)
            if r == 0:
                if h == 0:
                    split_factors(fv[:, rows], rows)
                counts_in(h, i).wait()
            log2_rate = jnp.dot(zs[rows, :], ls[:, columns], preferred_element_type=f32)
            intensity = jnp.exp2(log2_rate)
            count = cv[rows, columns].astype(f32)
            high, low = split(count - intensity)
            rh[rows, columns] = high
            rl[rows, columns] = low
            a = jnp.dot(zt[0:32, rows], high, preferred_element_type=f32)
            b = jnp.dot(zt[0:16, rows], low, preferred_element_type=f32)
            lacc[...] = (lacc[...] if i else 0.0) + (a[0:16] + a[16:32] + b)
            if r == 1:
                tacc[0] += jnp.sum((count * log2_rate).reshape(S // 8, 8, SH), axis=0)
                tacc[1] += jnp.sum(intensity.reshape(S // 8, 8, SH), axis=0)

    def factor_step_part(i):
        rows = slice(i * W, (i + 1) * W)
        a = lax.dot_general(lt[0:32], rh[rows, :], NT, preferred_element_type=f32)
        b = lax.dot_general(lt[0:16], rl[rows, :], NT, preferred_element_type=f32)
        fs[:, rows] = a[0:16] + a[16:32] + b

    def spread(source, target, send, recv, me, where):
        def copy(d):
            to = (me + d) % 8
            return remote(source, target.at[me], send.at[d], recv.at[me], where(to))

        def arrival(d):
            of = (me + d) % 8
            return remote(source, target.at[of], send.at[d], recv.at[of], where(of))

        def start():
            for d in range(1, 8):
                copy(d).start()
            target[me] = source[...]

        def wait():
            for d in range(1, 8):
                arrival(d).wait_recv()
            v = [target[p] for p in range(8)]
            return ((v[0] + v[1]) + (v[2] + v[3])) + ((v[4] + v[5]) + (v[6] + v[7]))

        def sent():
            for d in range(1, 8):
                copy(d).wait_send()

        return start, wait, sent

    def at_z(i):
        return {"z": i}

    def in_plane(r, h):
        return spread(sa.at[r, h], ra.at[r, h], asend.at[r, h, 0], arecv.at[r, h, 0], g, at_g)

    def along_z(r, h):
        return spread(sb.at[r, h], rb.at[r, h], asend.at[r, h, 1], arecv.at[r, h, 1], z, at_z)

    def sum_begin(r, h):
        sa[r, h] = lacc[...]
        in_plane(r, h)[0]()

    def sum_middle(r, h):
        sb[r, h] = in_plane(r, h)[1]()
        along_z(r, h)[0]()

    def sum_end(r, h):
        return along_z(r, h)[1]()

    def sum_sent(r, h):
        in_plane(r, h)[2]()
        along_z(r, h)[2]()

    def folded(value):
        rows, columns = value.shape
        total = jnp.zeros((8, 128), f32)
        for i in range(rows // 8):
            for j in range(columns // 128):
                total += value[8 * i : 8 * i + 8, 128 * j : 128 * j + 128]
        return total

    e_plane = spread(es.at[0], er.at[0], esend.at[0], erecv.at[0], g, at_g)
    e_line = spread(es.at[1], er.at[1], esend.at[1], erecv.at[1], z, at_z)
    sp_me = xl * 2 + core
    sp_others = (
        (other_core, xl * 2 + (1 - core)),
        (other_chip, (1 - xl) * 2 + core),
        (other_both, (1 - xl) * 2 + (1 - core)),
    )

    def sp_copy(e, d):
        return remote(es.at[e], er.at[e, sp_me], esend.at[e, d], erecv.at[e, sp_me], sp_others[d][0])

    def sp_begin(e, value):
        es[e] = value
        for d in range(3):
            sp_copy(e, d).start()
        er[e, sp_me] = value

    def sp_end(e):
        for d, (device, slot) in enumerate(sp_others):
            remote(es.at[e], er.at[e, slot], esend.at[e, d], erecv.at[e, slot], device).wait_recv()
        return (er[e, 0] + er[e, 1]) + (er[e, 2] + er[e, 3])

    def mine(i, who):
        return pl.ds(pl.multiple_of(i * W + who * H, H), H)

    def core_copy(r, i):
        return remote(fs.at[:, mine(i, 1 - core)], crecv.at[r, i],
                      fsend.at[r, 0, i], frecv.at[r, 0, i], other_core)

    def chip_copy(r, i):
        return remote(xs.at[i], xrecv.at[r, i],
                      fsend.at[r, 1, i], frecv.at[r, 1, i], other_chip)

    def back_copy(r, i):
        where = gs.at[r, :, mine(i, core)]
        return remote(where, where, fsend.at[r, 2, i], frecv.at[r, 2, i], other_core)

    def chip_sum(r, i):
        core_copy(r, i).wait_recv()
        xs[i] = fs[:, mine(i, core)] + crecv[r, i]
        chip_copy(r, i).start()

    def full_sum(r, i):
        chip_copy(r, i).wait_recv()
        gs[r, :, mine(i, core)] = xs[i] + xrecv[r, i]
        back_copy(r, i).start()

    def back_wait(r, i):
        remote(gs.at[r, :, mine(i, core)], gs.at[r, :, mine(i, 1 - core)],
               fsend.at[r, 2, i], frecv.at[r, 2, i], other_core).wait_recv()

    def exchange(r, between):
        for i in range(NW + 2):
            if i < NW:
                factor_step_part(i)
                core_copy(r, i).start()
            if 1 <= i < NW + 1:
                chip_sum(r, i - 1)
            if 2 <= i:
                full_sum(r, i - 2)
            between(i)
        for i in range(NW):
            back_wait(r, i)
            core_copy(r, i).wait_send()
            chip_copy(r, i).wait_send()
            back_copy(r, i).wait_send()

    tacc[...] = jnp.zeros_like(tacc)
    ins[0].wait()
    ins[1].wait()
    for h in range(2):
        split_loadings(lv[:, h * SH : (h + 1) * SH], h)
    residual_pass(0, 0)
    zp[0, :, pl.ds(128, CELLS)] = fv[...]
    pack_columns(0)
    pl.semaphore_wait(
        barrier, 17 + carry_left.astype(jnp.int32) + carry_right.astype(jnp.int32)
    )
    sum_begin(0, 0)
    send_rims(0)
    residual_pass(0, 1)
    sum_begin(0, 1)

    for copy in ins[2:]:
        copy.wait()
    step_f = fstep_ref[0]
    step_l = lstep_ref[0]
    row = lax.broadcasted_iota(jnp.int32, (K, 128), 0)
    gain = zeros
    for k in range(K):
        gain = jnp.where(row == k, prec_ref[k], gain)

    def prior_first():
        wait_rims(0)

        def body(j, carry):
            here = pl.ds(pl.multiple_of(j * 128, 128), 128)
            _, prior = prior_block(0, j)
            base[:, here] = fm[:, here] - (0.5 * step_f) * (gain * prior)
            return carry

        lax.fori_loop(0, NB, body, 0, unroll=8)

    def between_first(i):
        if i == 3:
            sum_middle(0, 0)
        if i == 5:
            prior_first()
        if i == 6:
            sum_middle(0, 1)

    exchange(0, between_first)

    half_now = base[...] + (0.5 * step_f) * gs[0]
    half[...] = half_now
    zp[1, :, pl.ds(128, CELLS)] = fv[...] + step_f * half_now
    pack_columns(1)
    send_rims(1)
    nf_out = pltpu.make_async_copy(zp.at[1, :, pl.ds(128, CELLS)], nf_hbm, osem.at[0])
    nf_out.start()
    split_factors(zp[1, :, pl.ds(128, CELLS)], slice(0, CELLS))

    for h in range(2):
        columns = slice(h * SH, (h + 1) * SH)
        half_l = lm[:, columns] + (0.5 * step_l) * (sum_end(0, h) - lv[:, columns])
        hl[:, columns] = half_l
        new_l = lv[:, columns] + step_l * half_l
        nl[:, columns] = new_l
        split_loadings(new_l, h)
        residual_pass(1, h)
        sum_begin(1, h)
    nl_out = pltpu.make_async_copy(nl, nl_hbm, osem.at[1])
    nl_out.start()
    sp_begin(2, folded(tacc[1] - LN2 * tacc[0]))

    def prior_second():
        wait_rims(1)

        def body(j, total):
            here = pl.ds(pl.multiple_of(j * 128, 128), 128)
            block, prior = prior_block(1, j)
            weighted = gain * prior
            base[:, here] = half[:, here] - (0.5 * step_f) * weighted
            return total + block * weighted

        ct[...] = lax.fori_loop(0, NB, body, zeros, unroll=8)

    def between_second(i):
        if i == 1:
            prior_second()
        if i == 3:
            sum_middle(1, 0)
        if i == 6:
            sum_middle(1, 1)

    exchange(1, between_second)

    end_f = base[...] + (0.5 * step_f) * gs[1]
    efac[...] = end_f
    es[0] = sp_end(2) + 0.5 * (folded(ct[...]) + folded(end_f * end_f))
    e_plane[0]()
    nfm_out = pltpu.make_async_copy(efac, nfm_hbm, osem.at[2])
    nfm_out.start()

    loading_terms = jnp.zeros((8, 128), f32)
    for h in range(2):
        columns = slice(h * SH, (h + 1) * SH)
        new_l = nl[:, columns]
        end_l = hl[:, columns] + (0.5 * step_l) * (sum_end(1, h) - new_l)
        elo[:, columns] = end_l
        loading_terms += folded(new_l * new_l) + folded(end_l * end_l)
    sp_begin(3, 0.5 * loading_terms)
    nlm_out = pltpu.make_async_copy(elo, nlm_hbm, osem.at[3])
    nlm_out.start()
    es[1] = e_plane[1]()
    e_line[0]()
    total = sp_end(3) + e_line[1]()
    en_ref[...] = total

    for r in range(2):
        for h in range(2):
            sum_sent(r, h)
    e_plane[2]()
    e_line[2]()
    for e in (2, 3):
        for d in range(3):
            sp_copy(e, d).wait_send()
    for copy in (nf_out, nl_out, nfm_out, nlm_out):
        copy.wait()


def keep(a, b, c, d, e, a_out, b_out, c_out, d_out, e_out, sem):
    pairs = ((a, a_out), (b, b_out), (c, c_out), (d, d_out))
    copies = [pltpu.make_async_copy(x, x_out, sem.at[i]) for i, (x, x_out) in enumerate(pairs)]
    for copy in copies:
        copy.start()
    e_out[0] = jnp.sum(e[...]) / TOTAL
    for copy in copies:
        copy.wait()


def local(
    counts, factors, loadings, factor_momenta, loading_momenta, precision, factor_step, loading_step
):
    hbm = pl.BlockSpec(memory_space=pl.ANY)
    smem = pl.BlockSpec(memory_space=pltpu.SMEM)
    vm = pltpu.VMEM
    dma = pltpu.SemaphoreType.DMA
    outs = pl.pallas_call(
        kernel,
        out_shape=(
            vm((K, CELLS), f32),
            vm((K, CELLS), f32),
            vm((K, SPEC), f32),
            vm((K, SPEC), f32),
            vm((8, 128), f32),
        ),
        in_specs=[hbm] * 8,
        out_specs=(pl.BlockSpec(memory_space=vm),) * 5,
        scratch_shapes=[
            pltpu.SMEM((K,), f32),
            pltpu.SMEM((1,), f32),
            pltpu.SMEM((1,), f32),
            vm((CELLS, SPEC), jnp.int32),
            vm((K, CELLS), f32),
            vm((K, SPEC), f32),
            vm((K, CELLS), f32),
            vm((K, SPEC), f32),
            vm((2, K, PAD), f32),
            vm((2, 2, K, 128), f32),
            vm((2, 2, K, 128), f32),
            vm((48, CELLS), bf16),
            vm((CELLS, 48), bf16),
            vm((48, SPEC), bf16),
            vm((32, SPEC), bf16),
            vm((CELLS, SPEC), bf16),
            vm((CELLS, SPEC), bf16),
            vm((K, SH), f32),
            vm((2, 8, SH), f32),
            vm((K, CELLS), f32),
            vm((2, NW, K, H), f32),
            vm((NW, K, H), f32),
            vm((2, NW, K, H), f32),
            vm((2, K, CELLS), f32),
            vm((K, CELLS), f32),
            vm((K, CELLS), f32),
            vm((K, CELLS), f32),
            vm((K, SPEC), f32),
            vm((K, SPEC), f32),
            vm((K, SPEC), f32),
            vm((K, 128), f32),
            vm((2, 2, K, SH), f32),
            vm((2, 2, 8, K, SH), f32),
            vm((2, 2, K, SH), f32),
            vm((2, 2, 8, K, SH), f32),
            vm((4, 8, 128), f32),
            vm((4, 8, 8, 128), f32),
            dma((2, NS)),
            dma((7,)),
            dma((4,)),
            dma((2, 4)),
            dma((2, 4)),
            dma((2, 2, 2, 8)),
            dma((2, 2, 2, 8)),
            dma((2, 3, NW)),
            dma((2, 3, NW)),
            dma((4, 8)),
            dma((4, 8)),
        ],
        compiler_params=pltpu.CompilerParams(
            collective_id=0, has_side_effects=True, vmem_limit_bytes=56 * 1024 * 1024
        ),
        name="leapfrog",
    )(
        counts[0], factors[0], loadings.T, factor_momenta[0], loading_momenta.T,
        precision, factor_step, loading_step,
    )
    new_factors, end_factor, new_loadings, end_loading, energy = pl.pallas_call(
        keep,
        out_shape=tuple(jax.ShapeDtypeStruct(x.shape, x.dtype) for x in outs[:4])
        + (jax.ShapeDtypeStruct((1,), f32),),
        in_specs=[pl.BlockSpec(memory_space=vm)] * 5,
        out_specs=(hbm,) * 4 + (smem,),
        scratch_shapes=[dma((4,))],
        compiler_params=pltpu.CompilerParams(vmem_limit_bytes=56 * 1024 * 1024),
        name="keep",
    )(*(pltpu.with_memory_space_constraint(x, vm) for x in outs))
    return new_factors[None], end_factor[None], new_loadings.T, end_loading.T, energy


def solution(mesh):
    torus = Mesh(mesh.devices.reshape(8, 2, 4, 2, 2), SITE + SP)
    placed = (
        P(SITE, None, SP),
        P(SITE, None, None),
        P(SP, None),
        P(SITE, None, None),
        P(SP, None),
        P(),
        P(),
        P(),
    )
    return jax.shard_map(
        local,
        mesh=torus,
        in_specs=placed,
        out_specs=(P(SITE, None, None), P(SITE, None, None), P(SP, None), P(SP, None), P()),
        check_vma=False,
    )
```

```python
import math

import jax
import jax.numpy as jnp
from jax import lax
from jax.experimental import pallas as pl
from jax.experimental.pallas import tpu as pltpu
from jax.sharding import Mesh
from jax.sharding import PartitionSpec as P

SITE = ("z", "xh", "y")
SP = ("xl", "core")
K = 16
TY = 64
CELLS = 5120
SPEC = 512
NZ = 8
NG = 8
TOTAL = 640 * 512 * 2048
S = 1280
NS = CELLS // S
SH = SPEC // 2
W = 1024
NW = CELLS // W
H = W // 2
NB = CELLS // 128
PAD = CELLS + 256
LOG2E = math.log2(math.e)
LN2 = math.log(2.0)
f32 = jnp.float32
bf16 = jnp.bfloat16
NT = (((1,), (1,)), ((), ()))
TN = (((0,), (0,)), ((), ()))


def split(value):
    high = value.astype(bf16)
    low = (value - high.astype(f32)).astype(bf16)
    return high, low


def lanes(shape=(K, 128)):
    return lax.broadcasted_iota(jnp.int32, shape, 1)


def kernel(
    counts_hbm, fac_hbm, ld_hbm, fmom_hbm, lmom_hbm, prec_hbm, fstep_hbm, lstep_hbm,
    nf_hbm, nfm_hbm, nl_hbm, nlm_hbm, en_ref,
    prec_ref, fstep_ref, lstep_ref,
    cv, fv, lv, fm, lm, zp, cols, halo, zt, zs, ls, lt, rh, rl, lacc, tacc,
    fs, crecv, xs, xrecv, gs, base, half, efac, nl, hl, elo, ct,
    sa, ra, sb, rb, es, er,
    csem, isem, osem, hsend, hrecv, asend, arecv, fsend, frecv, esend, erecv,
):
    z = lax.axis_index("z")
    xh = lax.axis_index("xh")
    y = lax.axis_index("y")
    xl = lax.axis_index("xl")
    core = lax.axis_index("core")
    g = xh * 4 + y
    site = z * NG + g

    def at_g(i):
        return {"xh": i // 4, "y": i % 4}

    def at_site(i):
        return {"z": i // NG, "xh": (i % NG) // 4, "y": i % 4}

    other_core = {"core": 1 - core}
    other_chip = {"xl": 1 - xl}
    other_both = {"xl": 1 - xl, "core": 1 - core}
    has_up, has_down = z > 0, z < NZ - 1
    has_left, has_right = site > 0, site < NZ * NG - 1
    carry_left = jnp.logical_and(g == 0, has_left)
    carry_right = jnp.logical_and(g == NG - 1, has_right)

    ins = [
        pltpu.make_async_copy(src, dst, isem.at[i])
        for i, (src, dst) in enumerate(
            (
                (fac_hbm, fv), (ld_hbm, lv), (fmom_hbm, fm), (lmom_hbm, lm),
                (prec_hbm, prec_ref), (fstep_hbm, fstep_ref), (lstep_hbm, lstep_ref),
            )
        )
    ]

    def counts_in(h, i):
        rows, columns = slice(i * S, (i + 1) * S), slice(h * SH, (h + 1) * SH)
        return pltpu.make_async_copy(
            counts_hbm.at[rows, columns], cv.at[rows, columns], csem.at[h, i]
        )

    ins[0].start()
    ins[1].start()
    for h in range(2):
        for i in range(NS):
            counts_in(h, i).start()
    for copy in ins[2:]:
        copy.start()

    barrier = pltpu.get_barrier_semaphore()

    def greet(device):
        pl.semaphore_signal(barrier, inc=1, device_id=device, device_id_type=pl.DeviceIdType.MESH)

    for device in (other_core, other_chip, other_both):
        greet(device)
    for d in range(1, NZ):
        greet({"z": (z + d) % NZ})
    for d in range(1, NG):
        greet(at_g((g + d) % NG))

    @pl.when(carry_left)
    def _():
        greet(at_site(site - 1))

    @pl.when(carry_right)
    def _():
        greet(at_site(site + 1))

    zeros = jnp.zeros((K, 128), f32)
    for r in range(2):

        @pl.when(jnp.logical_not(has_up))
        def _():
            zp[r, :, pl.ds(0, 128)] = zeros

        @pl.when(jnp.logical_not(has_down))
        def _():
            zp[r, :, pl.ds(PAD - 128, 128)] = zeros

        @pl.when(jnp.logical_not(has_left))
        def _():
            halo[r, 0] = zeros

        @pl.when(jnp.logical_not(has_right))
        def _():
            halo[r, 1] = zeros

    def remote(src, dst, send, recv, device):
        return pltpu.make_async_remote_copy(
            src_ref=src, dst_ref=dst, send_sem=send, recv_sem=recv,
            device_id=device, device_id_type=pl.DeviceIdType.MESH,
        )

    def pack_columns(r):
        def body(j, both):
            first, last = both
            block = zp[r, :, pl.ds(pl.multiple_of(128 + j * 128, 128), 128)]
            here = lanes() % TY == j
            first = jnp.where(here, pltpu.roll(block, j, 1), first)
            last = jnp.where(here, pltpu.roll(block, j + 65, 1), last)
            return first, last

        first, last = lax.fori_loop(0, NB, body, (zeros, zeros), unroll=8)
        cols[r, 0] = first
        cols[r, 1] = last

    def rim_copies(r):
        return (
            (
                has_down,
                has_up,
                remote(zp.at[r, :, pl.ds(PAD - 256, 128)], zp.at[r, :, pl.ds(0, 128)],
                       hsend.at[r, 0], hrecv.at[r, 0], {"z": lax.min(z + 1, NZ - 1)}),
            ),
            (
                has_up,
                has_down,
                remote(zp.at[r, :, pl.ds(128, 128)], zp.at[r, :, pl.ds(PAD - 128, 128)],
                       hsend.at[r, 1], hrecv.at[r, 1], {"z": lax.max(z - 1, 0)}),
            ),
            (
                has_right,
                has_left,
                remote(cols.at[r, 1], halo.at[r, 0], hsend.at[r, 2], hrecv.at[r, 2],
                       at_site(lax.min(site + 1, NZ * NG - 1))),
            ),
            (
                has_left,
                has_right,
                remote(cols.at[r, 0], halo.at[r, 1], hsend.at[r, 3], hrecv.at[r, 3],
                       at_site(lax.max(site - 1, 0))),
            ),
        )

    def send_rims(r):
        for sends, _, copy in rim_copies(r):
            pl.when(sends)(copy.start)

    def wait_rims(r):
        for sends, receives, copy in rim_copies(r):
            pl.when(sends)(copy.wait_send)
            pl.when(receives)(copy.wait_recv)

    def prior_block(r, j):
        def block_at(i):
            return zp[r, :, pl.ds(pl.multiple_of(i * 128, 128), 128)]

        before, block, after = block_at(j), block_at(j + 1), block_at(j + 2)
        lane = lanes()
        low = lane < TY
        up = pltpu.roll(jnp.where(low, block, before), TY, 1)
        down = pltpu.roll(jnp.where(low, after, block), TY, 1)
        left = jnp.where(
            lane % TY == 0, pltpu.roll(halo[r, 0], (128 - j) % 128, 1), pltpu.roll(block, 1, 1)
        )
        right = jnp.where(
            lane % TY == TY - 1, pltpu.roll(halo[r, 1], TY - 1 - j, 1), pltpu.roll(block, 127, 1)
        )
        return block, 4.25 * block - (up + down + left + right)

    def split_factors(value, rows):
        high, low = split(value)
        both = jnp.concatenate([high, low, high], axis=0)
        zt[:, rows] = both
        zs[rows, :] = both.T

    def split_loadings(value, h):
        columns = slice(h * SH, (h + 1) * SH)
        high, low = split(value * LOG2E)
        ls[0:16, columns] = high
        ls[16:32, columns] = high
        ls[32:48, columns] = low
        high, low = split(value)
        lt[0:16, columns] = high
        lt[16:32, columns] = low

    def residual_pass(r, h):
        columns = slice(h * SH, (h + 1) * SH)
        for i in range(NS):
            rows = slice(i * S, (i + 1) * S)
            if r == 0:
                if h == 0:
                    split_factors(fv[:, rows], rows)
                counts_in(h, i).wait()
            log2_rate = jnp.dot(zs[rows, :], ls[:, columns], preferred_element_type=f32)
            intensity = jnp.exp2(log2_rate)
            count = cv[rows, columns].astype(f32)
            high, low = split(count - intensity)
            rh[rows, columns] = high
            rl[rows, columns] = low
            a = jnp.dot(zt[0:32, rows], high, preferred_element_type=f32)
            b = jnp.dot(zt[0:16, rows], low, preferred_element_type=f32)
            lacc[...] = (lacc[...] if i else 0.0) + (a[0:16] + a[16:32] + b)
            if r == 1:
                tacc[0] += jnp.sum((count * log2_rate).reshape(S // 8, 8, SH), axis=0)
                tacc[1] += jnp.sum(intensity.reshape(S // 8, 8, SH), axis=0)

    def factor_step_part(i):
        rows = slice(i * W, (i + 1) * W)
        a = lax.dot_general(lt[0:32], rh[rows, :], NT, preferred_element_type=f32)
        b = lax.dot_general(lt[0:16], rl[rows, :], NT, preferred_element_type=f32)
        fs[:, rows] = a[0:16] + a[16:32] + b

    def spread(source, target, send, recv, me, where):
        def copy(d):
            to = (me + d) % 8
            return remote(source, target.at[me], send.at[d], recv.at[me], where(to))

        def arrival(d):
            of = (me + d) % 8
            return remote(source, target.at[of], send.at[d], recv.at[of], where(of))

        def start():
            for d in range(1, 8):
                copy(d).start()
            target[me] = source[...]

        def wait():
            for d in range(1, 8):
                arrival(d).wait_recv()
            v = [target[p] for p in range(8)]
            return ((v[0] + v[1]) + (v[2] + v[3])) + ((v[4] + v[5]) + (v[6] + v[7]))

        def sent():
            for d in range(1, 8):
                copy(d).wait_send()

        return start, wait, sent

    def at_z(i):
        return {"z": i}

    def in_plane(r, h):
        return spread(sa.at[r, h], ra.at[r, h], asend.at[r, h, 0], arecv.at[r, h, 0], g, at_g)

    def along_z(r, h):
        return spread(sb.at[r, h], rb.at[r, h], asend.at[r, h, 1], arecv.at[r, h, 1], z, at_z)

    def sum_begin(r, h):
        sa[r, h] = lacc[...]
        in_plane(r, h)[0]()

    def sum_middle(r, h):
        sb[r, h] = in_plane(r, h)[1]()
        along_z(r, h)[0]()

    def sum_end(r, h):
        return along_z(r, h)[1]()

    def sum_sent(r, h):
        in_plane(r, h)[2]()
        along_z(r, h)[2]()

    def folded(value):
        rows, columns = value.shape
        total = jnp.zeros((8, 128), f32)
        for i in range(rows // 8):
            for j in range(columns // 128):
                total += value[8 * i : 8 * i + 8, 128 * j : 128 * j + 128]
        return total

    e_plane = spread(es.at[0], er.at[0], esend.at[0], erecv.at[0], g, at_g)
    e_line = spread(es.at[1], er.at[1], esend.at[1], erecv.at[1], z, at_z)
    sp_me = xl * 2 + core
    sp_others = (
        (other_core, xl * 2 + (1 - core)),
        (other_chip, (1 - xl) * 2 + core),
        (other_both, (1 - xl) * 2 + (1 - core)),
    )

    def sp_copy(e, d):
        return remote(es.at[e], er.at[e, sp_me], esend.at[e, d], erecv.at[e, sp_me], sp_others[d][0])

    def sp_begin(e, value):
        es[e] = value
        for d in range(3):
            sp_copy(e, d).start()
        er[e, sp_me] = value

    def sp_end(e):
        for d, (device, slot) in enumerate(sp_others):
            remote(es.at[e], er.at[e, slot], esend.at[e, d], erecv.at[e, slot], device).wait_recv()
        return (er[e, 0] + er[e, 1]) + (er[e, 2] + er[e, 3])

    def mine(i, who):
        return pl.ds(pl.multiple_of(i * W + who * H, H), H)

    def core_copy(r, i):
        return remote(fs.at[:, mine(i, 1 - core)], crecv.at[r, i],
                      fsend.at[r, 0, i], frecv.at[r, 0, i], other_core)

    def chip_copy(r, i):
        return remote(xs.at[i], xrecv.at[r, i],
                      fsend.at[r, 1, i], frecv.at[r, 1, i], other_chip)

    def back_copy(r, i):
        where = gs.at[r, :, mine(i, core)]
        return remote(where, where, fsend.at[r, 2, i], frecv.at[r, 2, i], other_core)

    def chip_sum(r, i):
        core_copy(r, i).wait_recv()
        xs[i] = fs[:, mine(i, core)] + crecv[r, i]
        chip_copy(r, i).start()

    def full_sum(r, i):
        chip_copy(r, i).wait_recv()
        gs[r, :, mine(i, core)] = xs[i] + xrecv[r, i]
        back_copy(r, i).start()

    def back_wait(r, i):
        remote(gs.at[r, :, mine(i, core)], gs.at[r, :, mine(i, 1 - core)],
               fsend.at[r, 2, i], frecv.at[r, 2, i], other_core).wait_recv()

    def exchange(r, between):
        for i in range(NW):
            factor_step_part(i)
            core_copy(r, i).start()
            if i:
                chip_sum(r, i - 1)
            between(i)
        chip_sum(r, NW - 1)
        for i in range(NW):
            full_sum(r, i)
            between(NW + i)
        for i in range(NW):
            back_wait(r, i)

    def exchange_sent(r):
        for i in range(NW):
            core_copy(r, i).wait_send()
            chip_copy(r, i).wait_send()
            back_copy(r, i).wait_send()

    tacc[...] = jnp.zeros_like(tacc)
    ins[0].wait()
    ins[1].wait()
    for h in range(2):
        split_loadings(lv[:, h * SH : (h + 1) * SH], h)
    residual_pass(0, 0)
    pl.semaphore_wait(
        barrier, 17 + carry_left.astype(jnp.int32) + carry_right.astype(jnp.int32)
    )
    sum_begin(0, 0)
    residual_pass(0, 1)
    sum_begin(0, 1)
    zp[0, :, pl.ds(128, CELLS)] = fv[...]
    pack_columns(0)
    send_rims(0)

    for copy in ins[2:]:
        copy.wait()
    step_f = fstep_ref[0]
    step_l = lstep_ref[0]
    row = lax.broadcasted_iota(jnp.int32, (K, 128), 0)
    gain = zeros
    for k in range(K):
        gain = jnp.where(row == k, prec_ref[k], gain)

    def prior_first():
        wait_rims(0)

        def body(j, carry):
            here = pl.ds(pl.multiple_of(j * 128, 128), 128)
            _, prior = prior_block(0, j)
            base[:, here] = fm[:, here] - (0.5 * step_f) * (gain * prior)
            return carry

        lax.fori_loop(0, NB, body, 0, unroll=8)

    def between_first(i):
        if i == 3:
            sum_middle(0, 0)
        if i == 4:
            prior_first()
        if i == 6:
            sum_middle(0, 1)

    exchange(0, between_first)

    half_now = base[...] + (0.5 * step_f) * gs[0]
    half[...] = half_now
    zp[1, :, pl.ds(128, CELLS)] = fv[...] + step_f * half_now
    pack_columns(1)
    send_rims(1)
    nf_out = pltpu.make_async_copy(zp.at[1, :, pl.ds(128, CELLS)], nf_hbm, osem.at[0])
    nf_out.start()
    split_factors(zp[1, :, pl.ds(128, CELLS)], slice(0, CELLS))
    exchange_sent(0)

    for h in range(2):
        columns = slice(h * SH, (h + 1) * SH)
        half_l = lm[:, columns] + (0.5 * step_l) * (sum_end(0, h) - lv[:, columns])
        hl[:, columns] = half_l
        new_l = lv[:, columns] + step_l * half_l
        nl[:, columns] = new_l
        split_loadings(new_l, h)
        residual_pass(1, h)
        sum_begin(1, h)
    nl_out = pltpu.make_async_copy(nl, nl_hbm, osem.at[1])
    nl_out.start()
    sp_begin(2, folded(tacc[1] - LN2 * tacc[0]))

    def prior_second():
        wait_rims(1)

        def body(j, total):
            here = pl.ds(pl.multiple_of(j * 128, 128), 128)
            block, prior = prior_block(1, j)
            weighted = gain * prior
            base[:, here] = half[:, here] - (0.5 * step_f) * weighted
            return total + block * weighted

        ct[...] = lax.fori_loop(0, NB, body, zeros, unroll=8)

    def between_second(i):
        if i == 1:
            prior_second()
        if i == 3:
            sum_middle(1, 0)
        if i == 6:
            sum_middle(1, 1)

    exchange(1, between_second)

    end_f = base[...] + (0.5 * step_f) * gs[1]
    efac[...] = end_f
    es[0] = sp_end(2) + 0.5 * (folded(ct[...]) + folded(end_f * end_f))
    e_plane[0]()
    nfm_out = pltpu.make_async_copy(efac, nfm_hbm, osem.at[2])
    nfm_out.start()
    exchange_sent(1)
    for h in range(2):
        sum_sent(0, h)
    for d in range(3):
        sp_copy(2, d).wait_send()

    loading_terms = jnp.zeros((8, 128), f32)
    for h in range(2):
        columns = slice(h * SH, (h + 1) * SH)
        new_l = nl[:, columns]
        end_l = hl[:, columns] + (0.5 * step_l) * (sum_end(1, h) - new_l)
        elo[:, columns] = end_l
        loading_terms += folded(new_l * new_l) + folded(end_l * end_l)
    sp_begin(3, 0.5 * loading_terms)
    nlm_out = pltpu.make_async_copy(elo, nlm_hbm, osem.at[3])
    nlm_out.start()
    for h in range(2):
        sum_sent(1, h)
    es[1] = e_plane[1]()
    e_line[0]()
    e_plane[2]()
    for d in range(3):
        sp_copy(3, d).wait_send()
    for copy in (nf_out, nl_out, nfm_out, nlm_out):
        copy.wait()
    e_line[2]()
    total = sp_end(3) + e_line[1]()
    en_ref[...] = total


def keep(a, b, c, d, e, a_out, b_out, c_out, d_out, e_out, sem):
    pairs = ((a, a_out), (b, b_out), (c, c_out), (d, d_out))
    copies = [pltpu.make_async_copy(x, x_out, sem.at[i]) for i, (x, x_out) in enumerate(pairs)]
    for copy in copies:
        copy.start()
    e_out[0] = jnp.sum(e[...]) / TOTAL
    for copy in copies:
        copy.wait()


def local(
    counts, factors, loadings, factor_momenta, loading_momenta, precision, factor_step, loading_step
):
    hbm = pl.BlockSpec(memory_space=pl.ANY)
    smem = pl.BlockSpec(memory_space=pltpu.SMEM)
    vm = pltpu.VMEM
    dma = pltpu.SemaphoreType.DMA
    outs = pl.pallas_call(
        kernel,
        out_shape=(
            vm((K, CELLS), f32),
            vm((K, CELLS), f32),
            vm((K, SPEC), f32),
            vm((K, SPEC), f32),
            vm((8, 128), f32),
        ),
        in_specs=[hbm] * 8,
        out_specs=(pl.BlockSpec(memory_space=vm),) * 5,
        scratch_shapes=[
            pltpu.SMEM((K,), f32),
            pltpu.SMEM((1,), f32),
            pltpu.SMEM((1,), f32),
            vm((CELLS, SPEC), jnp.int32),
            vm((K, CELLS), f32),
            vm((K, SPEC), f32),
            vm((K, CELLS), f32),
            vm((K, SPEC), f32),
            vm((2, K, PAD), f32),
            vm((2, 2, K, 128), f32),
            vm((2, 2, K, 128), f32),
            vm((48, CELLS), bf16),
            vm((CELLS, 48), bf16),
            vm((48, SPEC), bf16),
            vm((32, SPEC), bf16),
            vm((CELLS, SPEC), bf16),
            vm((CELLS, SPEC), bf16),
            vm((K, SH), f32),
            vm((2, 8, SH), f32),
            vm((K, CELLS), f32),
            vm((2, NW, K, H), f32),
            vm((NW, K, H), f32),
            vm((2, NW, K, H), f32),
            vm((2, K, CELLS), f32),
            vm((K, CELLS), f32),
            vm((K, CELLS), f32),
            vm((K, CELLS), f32),
            vm((K, SPEC), f32),
            vm((K, SPEC), f32),
            vm((K, SPEC), f32),
            vm((K, 128), f32),
            vm((2, 2, K, SH), f32),
            vm((2, 2, 8, K, SH), f32),
            vm((2, 2, K, SH), f32),
            vm((2, 2, 8, K, SH), f32),
            vm((4, 8, 128), f32),
            vm((4, 8, 8, 128), f32),
            dma((2, NS)),
            dma((7,)),
            dma((4,)),
            dma((2, 4)),
            dma((2, 4)),
            dma((2, 2, 2, 8)),
            dma((2, 2, 2, 8)),
            dma((2, 3, NW)),
            dma((2, 3, NW)),
            dma((4, 8)),
            dma((4, 8)),
        ],
        compiler_params=pltpu.CompilerParams(
            collective_id=0, has_side_effects=True, vmem_limit_bytes=56 * 1024 * 1024
        ),
        name="leapfrog",
    )(
        counts[0], factors[0], loadings.T, factor_momenta[0], loading_momenta.T,
        precision, factor_step, loading_step,
    )
    new_factors, end_factor, new_loadings, end_loading, energy = pl.pallas_call(
        keep,
        out_shape=tuple(jax.ShapeDtypeStruct(x.shape, x.dtype) for x in outs[:4])
        + (jax.ShapeDtypeStruct((1,), f32),),
        in_specs=[pl.BlockSpec(memory_space=vm)] * 5,
        out_specs=(hbm,) * 4 + (smem,),
        scratch_shapes=[dma((4,))],
        compiler_params=pltpu.CompilerParams(vmem_limit_bytes=56 * 1024 * 1024),
        name="keep",
    )(*(pltpu.with_memory_space_constraint(x, vm) for x in outs))
    return new_factors[None], end_factor[None], new_loadings.T, end_loading.T, energy


def solution(mesh):
    torus = Mesh(mesh.devices.reshape(8, 2, 4, 2, 2), SITE + SP)
    placed = (
        P(SITE, None, SP),
        P(SITE, None, None),
        P(SP, None),
        P(SITE, None, None),
        P(SP, None),
        P(),
        P(),
        P(),
    )
    return jax.shard_map(
        local,
        mesh=torus,
        in_specs=placed,
        out_specs=(P(SITE, None, None), P(SITE, None, None), P(SP, None), P(SP, None), P()),
        check_vma=False,
    )
```

```python
import math

import jax
import jax.numpy as jnp
from jax import lax
from jax.experimental import pallas as pl
from jax.experimental.pallas import tpu as pltpu
from jax.sharding import Mesh
from jax.sharding import PartitionSpec as P

SITE = ("z", "xh", "y")
SP = ("xl", "core")
K = 16
TY = 64
CELLS = 5120
SPEC = 512
NZ = 8
NG = 8
TOTAL = 640 * 512 * 2048
S = 1280
NS = CELLS // S
SH = SPEC // 2
W = 1024
NW = CELLS // W
H = W // 2
NB = CELLS // 128
PAD = CELLS + 256
LOG2E = math.log2(math.e)
LN2 = math.log(2.0)
f32 = jnp.float32
bf16 = jnp.bfloat16
NT = (((1,), (1,)), ((), ()))
TN = (((0,), (0,)), ((), ()))


def split(value):
    high = value.astype(bf16)
    low = (value - high.astype(f32)).astype(bf16)
    return high, low


def lanes(shape=(K, 128)):
    return lax.broadcasted_iota(jnp.int32, shape, 1)


def kernel(
    counts_hbm, fac_hbm, ld_hbm, fmom_hbm, lmom_hbm, prec_hbm, fstep_hbm, lstep_hbm,
    nf_hbm, nfm_hbm, nl_hbm, nlm_hbm, en_ref,
    prec_ref, fstep_ref, lstep_ref,
    cv, fv, lv, fm, lm, zp, cols, halo, zt, zs, ls, lt, rh, rl, lacc, tacc,
    fs, crecv, xs, xrecv, gs, base, half, efac, nl, hl, elo, ct,
    sa, ra, sb, rb, es, er,
    csem, isem, osem, hsend, hrecv, asend, arecv, fsend, frecv, esend, erecv,
):
    z = lax.axis_index("z")
    xh = lax.axis_index("xh")
    y = lax.axis_index("y")
    xl = lax.axis_index("xl")
    core = lax.axis_index("core")
    g = xh * 4 + y
    site = z * NG + g

    def at_g(i):
        return {"xh": i // 4, "y": i % 4}

    def at_site(i):
        return {"z": i // NG, "xh": (i % NG) // 4, "y": i % 4}

    other_core = {"core": 1 - core}
    other_chip = {"xl": 1 - xl}
    other_both = {"xl": 1 - xl, "core": 1 - core}
    has_up, has_down = z > 0, z < NZ - 1
    has_left, has_right = site > 0, site < NZ * NG - 1
    carry_left = jnp.logical_and(g == 0, has_left)
    carry_right = jnp.logical_and(g == NG - 1, has_right)

    ins = [
        pltpu.make_async_copy(src, dst, isem.at[i])
        for i, (src, dst) in enumerate(
            (
                (fac_hbm, fv), (ld_hbm, lv), (fmom_hbm, fm), (lmom_hbm, lm),
                (prec_hbm, prec_ref), (fstep_hbm, fstep_ref), (lstep_hbm, lstep_ref),
            )
        )
    ]

    def counts_in(h, i):
        rows, columns = slice(i * S, (i + 1) * S), slice(h * SH, (h + 1) * SH)
        return pltpu.make_async_copy(
            counts_hbm.at[rows, columns], cv.at[rows, columns], csem.at[h, i]
        )

    ins[0].start()
    ins[1].start()
    for h in range(2):
        for i in range(NS):
            counts_in(h, i).start()
    for copy in ins[2:]:
        copy.start()

    barrier = pltpu.get_barrier_semaphore()

    def greet(device):
        pl.semaphore_signal(barrier, inc=1, device_id=device, device_id_type=pl.DeviceIdType.MESH)

    for device in (other_core, other_chip, other_both):
        greet(device)
    for d in range(1, NZ):
        greet({"z": (z + d) % NZ})
    for d in range(1, NG):
        greet(at_g((g + d) % NG))

    @pl.when(carry_left)
    def _():
        greet(at_site(site - 1))

    @pl.when(carry_right)
    def _():
        greet(at_site(site + 1))

    zeros = jnp.zeros((K, 128), f32)
    for r in range(2):

        @pl.when(jnp.logical_not(has_up))
        def _():
            zp[r, :, pl.ds(0, 128)] = zeros

        @pl.when(jnp.logical_not(has_down))
        def _():
            zp[r, :, pl.ds(PAD - 128, 128)] = zeros

        @pl.when(jnp.logical_not(has_left))
        def _():
            halo[r, 0] = zeros

        @pl.when(jnp.logical_not(has_right))
        def _():
            halo[r, 1] = zeros

    def remote(src, dst, send, recv, device):
        return pltpu.make_async_remote_copy(
            src_ref=src, dst_ref=dst, send_sem=send, recv_sem=recv,
            device_id=device, device_id_type=pl.DeviceIdType.MESH,
        )

    def pack_columns(r):
        def body(j, both):
            first, last = both
            block = zp[r, :, pl.ds(pl.multiple_of(128 + j * 128, 128), 128)]
            here = lanes() % TY == j
            first = jnp.where(here, pltpu.roll(block, j, 1), first)
            last = jnp.where(here, pltpu.roll(block, j + 65, 1), last)
            return first, last

        first, last = lax.fori_loop(0, NB, body, (zeros, zeros), unroll=8)
        cols[r, 0] = first
        cols[r, 1] = last

    def rim_copies(r):
        return (
            (
                has_down,
                has_up,
                remote(zp.at[r, :, pl.ds(PAD - 256, 128)], zp.at[r, :, pl.ds(0, 128)],
                       hsend.at[r, 0], hrecv.at[r, 0], {"z": lax.min(z + 1, NZ - 1)}),
            ),
            (
                has_up,
                has_down,
                remote(zp.at[r, :, pl.ds(128, 128)], zp.at[r, :, pl.ds(PAD - 128, 128)],
                       hsend.at[r, 1], hrecv.at[r, 1], {"z": lax.max(z - 1, 0)}),
            ),
            (
                has_right,
                has_left,
                remote(cols.at[r, 1], halo.at[r, 0], hsend.at[r, 2], hrecv.at[r, 2],
                       at_site(lax.min(site + 1, NZ * NG - 1))),
            ),
            (
                has_left,
                has_right,
                remote(cols.at[r, 0], halo.at[r, 1], hsend.at[r, 3], hrecv.at[r, 3],
                       at_site(lax.max(site - 1, 0))),
            ),
        )

    def send_rims(r):
        for sends, _, copy in rim_copies(r):
            pl.when(sends)(copy.start)

    def wait_rims(r):
        for sends, receives, copy in rim_copies(r):
            pl.when(sends)(copy.wait_send)
            pl.when(receives)(copy.wait_recv)

    def prior_block(r, j):
        def block_at(i):
            return zp[r, :, pl.ds(pl.multiple_of(i * 128, 128), 128)]

        before, block, after = block_at(j), block_at(j + 1), block_at(j + 2)
        lane = lanes()
        low = lane < TY
        up = pltpu.roll(jnp.where(low, block, before), TY, 1)
        down = pltpu.roll(jnp.where(low, after, block), TY, 1)
        left = jnp.where(
            lane % TY == 0, pltpu.roll(halo[r, 0], (128 - j) % 128, 1), pltpu.roll(block, 1, 1)
        )
        right = jnp.where(
            lane % TY == TY - 1, pltpu.roll(halo[r, 1], TY - 1 - j, 1), pltpu.roll(block, 127, 1)
        )
        return block, 4.25 * block - (up + down + left + right)

    def split_factors(value, rows):
        high, low = split(value)
        both = jnp.concatenate([high, low, high], axis=0)
        zt[:, rows] = both
        zs[rows, :] = both.T

    def split_loadings(value, h):
        columns = slice(h * SH, (h + 1) * SH)
        high, low = split(value * LOG2E)
        ls[0:16, columns] = high
        ls[16:32, columns] = high
        ls[32:48, columns] = low
        high, low = split(value)
        lt[0:16, columns] = high
        lt[16:32, columns] = low

    def residual_pass(r, h):
        columns = slice(h * SH, (h + 1) * SH)
        for i in range(NS):
            rows = slice(i * S, (i + 1) * S)
            if r == 0:
                if h == 0:
                    split_factors(fv[:, rows], rows)
                counts_in(h, i).wait()
            log2_rate = jnp.dot(zs[rows, :], ls[:, columns], preferred_element_type=f32)
            intensity = jnp.exp2(log2_rate)
            count = cv[rows, columns].astype(f32)
            high, low = split(count - intensity)
            rh[rows, columns] = high
            rl[rows, columns] = low
            a = jnp.dot(zt[0:32, rows], high, preferred_element_type=f32)
            b = jnp.dot(zt[0:16, rows], low, preferred_element_type=f32)
            lacc[...] = (lacc[...] if i else 0.0) + (a[0:16] + a[16:32] + b)
            if r == 1:
                tacc[0] += jnp.sum((count * log2_rate).reshape(S // 8, 8, SH), axis=0)
                tacc[1] += jnp.sum(intensity.reshape(S // 8, 8, SH), axis=0)

    def factor_step_part(i):
        rows = slice(i * W, (i + 1) * W)
        a = lax.dot_general(lt[0:32], rh[rows, :], NT, preferred_element_type=f32)
        b = lax.dot_general(lt[0:16], rl[rows, :], NT, preferred_element_type=f32)
        fs[:, rows] = a[0:16] + a[16:32] + b

    def spread(source, target, send, recv, me, where):
        def copy(d):
            to = (me + d) % 8
            return remote(source, target.at[me], send.at[d], recv.at[me], where(to))

        def arrival(d):
            of = (me + d) % 8
            return remote(source, target.at[of], send.at[d], recv.at[of], where(of))

        def start():
            for d in range(1, 8):
                copy(d).start()
            target[me] = source[...]

        def wait():
            for d in range(1, 8):
                arrival(d).wait_recv()
            v = [target[p] for p in range(8)]
            return ((v[0] + v[1]) + (v[2] + v[3])) + ((v[4] + v[5]) + (v[6] + v[7]))

        def sent():
            for d in range(1, 8):
                copy(d).wait_send()

        return start, wait, sent

    def at_z(i):
        return {"z": i}

    def in_plane(r, h):
        return spread(sa.at[r, h], ra.at[r, h], asend.at[r, h, 0], arecv.at[r, h, 0], g, at_g)

    def along_z(r, h):
        return spread(sb.at[r, h], rb.at[r, h], asend.at[r, h, 1], arecv.at[r, h, 1], z, at_z)

    def sum_begin(r, h):
        sa[r, h] = lacc[...]
        in_plane(r, h)[0]()

    def sum_middle(r, h):
        sb[r, h] = in_plane(r, h)[1]()
        along_z(r, h)[0]()

    def sum_end(r, h):
        return along_z(r, h)[1]()

    def sum_sent(r, h):
        in_plane(r, h)[2]()
        along_z(r, h)[2]()

    def folded(value):
        rows, columns = value.shape
        total = jnp.zeros((8, 128), f32)
        for i in range(rows // 8):
            for j in range(columns // 128):
                total += value[8 * i : 8 * i + 8, 128 * j : 128 * j + 128]
        return total

    e_plane = spread(es.at[0], er.at[0], esend.at[0], erecv.at[0], g, at_g)
    e_line = spread(es.at[1], er.at[1], esend.at[1], erecv.at[1], z, at_z)
    sp_me = xl * 2 + core
    sp_others = (
        (other_core, xl * 2 + (1 - core)),
        (other_chip, (1 - xl) * 2 + core),
        (other_both, (1 - xl) * 2 + (1 - core)),
    )

    def sp_copy(e, d):
        return remote(es.at[e], er.at[e, sp_me], esend.at[e, d], erecv.at[e, sp_me], sp_others[d][0])

    def sp_begin(e, value):
        es[e] = value
        for d in range(3):
            sp_copy(e, d).start()
        er[e, sp_me] = value

    def sp_end(e):
        for d, (device, slot) in enumerate(sp_others):
            remote(es.at[e], er.at[e, slot], esend.at[e, d], erecv.at[e, slot], device).wait_recv()
        return (er[e, 0] + er[e, 1]) + (er[e, 2] + er[e, 3])

    def mine(i, who):
        return pl.ds(pl.multiple_of(i * W + who * H, H), H)

    def core_copy(r, i):
        return remote(fs.at[:, mine(i, 1 - core)], crecv.at[r, i],
                      fsend.at[r, 0, i], frecv.at[r, 0, i], other_core)

    def chip_copy(r, i):
        return remote(xs.at[i], xrecv.at[r, i],
                      fsend.at[r, 1, i], frecv.at[r, 1, i], other_chip)

    def back_copy(r, i):
        where = gs.at[r, :, mine(i, core)]
        return remote(where, where, fsend.at[r, 2, i], frecv.at[r, 2, i], other_core)

    def chip_sum(r, i):
        core_copy(r, i).wait_recv()
        xs[i] = fs[:, mine(i, core)] + crecv[r, i]
        chip_copy(r, i).start()

    def full_sum(r, i):
        chip_copy(r, i).wait_recv()
        gs[r, :, mine(i, core)] = xs[i] + xrecv[r, i]
        back_copy(r, i).start()

    def back_wait(r, i):
        remote(gs.at[r, :, mine(i, core)], gs.at[r, :, mine(i, 1 - core)],
               fsend.at[r, 2, i], frecv.at[r, 2, i], other_core).wait_recv()

    def exchange(r, between):
        for i in range(NW):
            factor_step_part(i)
            core_copy(r, i).start()
            if i >= 2:
                chip_sum(r, i - 2)
            between(i)
        chip_sum(r, NW - 2)
        chip_sum(r, NW - 1)
        for i in range(NW):
            full_sum(r, i)
            between(NW + i)
        for i in range(NW):
            back_wait(r, i)

    def exchange_sent(r):
        for i in range(NW):
            core_copy(r, i).wait_send()
            chip_copy(r, i).wait_send()
            back_copy(r, i).wait_send()

    tacc[...] = jnp.zeros_like(tacc)
    ins[0].wait()
    ins[1].wait()
    for h in range(2):
        split_loadings(lv[:, h * SH : (h + 1) * SH], h)
    residual_pass(0, 0)
    pl.semaphore_wait(
        barrier, 17 + carry_left.astype(jnp.int32) + carry_right.astype(jnp.int32)
    )
    sum_begin(0, 0)
    residual_pass(0, 1)
    sum_begin(0, 1)
    zp[0, :, pl.ds(128, CELLS)] = fv[...]
    pack_columns(0)
    send_rims(0)

    for copy in ins[2:]:
        copy.wait()
    step_f = fstep_ref[0]
    step_l = lstep_ref[0]
    row = lax.broadcasted_iota(jnp.int32, (K, 128), 0)
    gain = zeros
    for k in range(K):
        gain = jnp.where(row == k, prec_ref[k], gain)

    def prior_first():
        wait_rims(0)

        def body(j, carry):
            here = pl.ds(pl.multiple_of(j * 128, 128), 128)
            _, prior = prior_block(0, j)
            base[:, here] = fm[:, here] - (0.5 * step_f) * (gain * prior)
            return carry

        lax.fori_loop(0, NB, body, 0, unroll=8)

    def between_first(i):
        if i == 4:
            sum_middle(0, 0)
        if i == 5:
            prior_first()
        if i == 6:
            sum_middle(0, 1)

    exchange(0, between_first)

    half_now = base[...] + (0.5 * step_f) * gs[0]
    half[...] = half_now
    zp[1, :, pl.ds(128, CELLS)] = fv[...] + step_f * half_now
    pack_columns(1)
    send_rims(1)
    nf_out = pltpu.make_async_copy(zp.at[1, :, pl.ds(128, CELLS)], nf_hbm, osem.at[0])
    nf_out.start()
    split_factors(zp[1, :, pl.ds(128, CELLS)], slice(0, CELLS))
    exchange_sent(0)

    for h in range(2):
        columns = slice(h * SH, (h + 1) * SH)
        half_l = lm[:, columns] + (0.5 * step_l) * (sum_end(0, h) - lv[:, columns])
        hl[:, columns] = half_l
        new_l = lv[:, columns] + step_l * half_l
        nl[:, columns] = new_l
        split_loadings(new_l, h)
        residual_pass(1, h)
        sum_begin(1, h)
    nl_out = pltpu.make_async_copy(nl, nl_hbm, osem.at[1])
    nl_out.start()
    sp_begin(2, folded(tacc[1] - LN2 * tacc[0]))

    def prior_second():
        wait_rims(1)

        def body(j, total):
            here = pl.ds(pl.multiple_of(j * 128, 128), 128)
            block, prior = prior_block(1, j)
            weighted = gain * prior
            base[:, here] = half[:, here] - (0.5 * step_f) * weighted
            return total + block * weighted

        ct[...] = lax.fori_loop(0, NB, body, zeros, unroll=8)

    def between_second(i):
        if i == 4:
            sum_middle(1, 0)
        if i == 5:
            prior_second()
        if i == 6:
            sum_middle(1, 1)

    exchange(1, between_second)

    end_f = base[...] + (0.5 * step_f) * gs[1]
    efac[...] = end_f
    es[0] = sp_end(2) + 0.5 * (folded(ct[...]) + folded(end_f * end_f))
    e_plane[0]()
    nfm_out = pltpu.make_async_copy(efac, nfm_hbm, osem.at[2])
    nfm_out.start()
    exchange_sent(1)
    for h in range(2):
        sum_sent(0, h)
    for d in range(3):
        sp_copy(2, d).wait_send()

    loading_terms = jnp.zeros((8, 128), f32)
    for h in range(2):
        columns = slice(h * SH, (h + 1) * SH)
        new_l = nl[:, columns]
        end_l = hl[:, columns] + (0.5 * step_l) * (sum_end(1, h) - new_l)
        elo[:, columns] = end_l
        loading_terms += folded(new_l * new_l) + folded(end_l * end_l)
    sp_begin(3, 0.5 * loading_terms)
    nlm_out = pltpu.make_async_copy(elo, nlm_hbm, osem.at[3])
    nlm_out.start()
    for h in range(2):
        sum_sent(1, h)
    es[1] = e_plane[1]()
    e_line[0]()
    e_plane[2]()
    for d in range(3):
        sp_copy(3, d).wait_send()
    for copy in (nf_out, nl_out, nfm_out, nlm_out):
        copy.wait()
    e_line[2]()
    total = sp_end(3) + e_line[1]()
    en_ref[...] = total


def keep(a, b, c, d, e, a_out, b_out, c_out, d_out, e_out, sem):
    pairs = ((a, a_out), (b, b_out), (c, c_out), (d, d_out))
    copies = [pltpu.make_async_copy(x, x_out, sem.at[i]) for i, (x, x_out) in enumerate(pairs)]
    for copy in copies:
        copy.start()
    e_out[0] = jnp.sum(e[...]) / TOTAL
    for copy in copies:
        copy.wait()


def local(
    counts, factors, loadings, factor_momenta, loading_momenta, precision, factor_step, loading_step
):
    hbm = pl.BlockSpec(memory_space=pl.ANY)
    smem = pl.BlockSpec(memory_space=pltpu.SMEM)
    vm = pltpu.VMEM
    dma = pltpu.SemaphoreType.DMA
    outs = pl.pallas_call(
        kernel,
        out_shape=(
            vm((K, CELLS), f32),
            vm((K, CELLS), f32),
            vm((K, SPEC), f32),
            vm((K, SPEC), f32),
            vm((8, 128), f32),
        ),
        in_specs=[hbm] * 8,
        out_specs=(pl.BlockSpec(memory_space=vm),) * 5,
        scratch_shapes=[
            pltpu.SMEM((K,), f32),
            pltpu.SMEM((1,), f32),
            pltpu.SMEM((1,), f32),
            vm((CELLS, SPEC), jnp.int32),
            vm((K, CELLS), f32),
            vm((K, SPEC), f32),
            vm((K, CELLS), f32),
            vm((K, SPEC), f32),
            vm((2, K, PAD), f32),
            vm((2, 2, K, 128), f32),
            vm((2, 2, K, 128), f32),
            vm((48, CELLS), bf16),
            vm((CELLS, 48), bf16),
            vm((48, SPEC), bf16),
            vm((32, SPEC), bf16),
            vm((CELLS, SPEC), bf16),
            vm((CELLS, SPEC), bf16),
            vm((K, SH), f32),
            vm((2, 8, SH), f32),
            vm((K, CELLS), f32),
            vm((2, NW, K, H), f32),
            vm((NW, K, H), f32),
            vm((2, NW, K, H), f32),
            vm((2, K, CELLS), f32),
            vm((K, CELLS), f32),
            vm((K, CELLS), f32),
            vm((K, CELLS), f32),
            vm((K, SPEC), f32),
            vm((K, SPEC), f32),
            vm((K, SPEC), f32),
            vm((K, 128), f32),
            vm((2, 2, K, SH), f32),
            vm((2, 2, 8, K, SH), f32),
            vm((2, 2, K, SH), f32),
            vm((2, 2, 8, K, SH), f32),
            vm((4, 8, 128), f32),
            vm((4, 8, 8, 128), f32),
            dma((2, NS)),
            dma((7,)),
            dma((4,)),
            dma((2, 4)),
            dma((2, 4)),
            dma((2, 2, 2, 8)),
            dma((2, 2, 2, 8)),
            dma((2, 3, NW)),
            dma((2, 3, NW)),
            dma((4, 8)),
            dma((4, 8)),
        ],
        compiler_params=pltpu.CompilerParams(
            collective_id=0, has_side_effects=True, vmem_limit_bytes=56 * 1024 * 1024
        ),
        name="leapfrog",
    )(
        counts[0], factors[0], loadings.T, factor_momenta[0], loading_momenta.T,
        precision, factor_step, loading_step,
    )
    new_factors, end_factor, new_loadings, end_loading, energy = pl.pallas_call(
        keep,
        out_shape=tuple(jax.ShapeDtypeStruct(x.shape, x.dtype) for x in outs[:4])
        + (jax.ShapeDtypeStruct((1,), f32),),
        in_specs=[pl.BlockSpec(memory_space=vm)] * 5,
        out_specs=(hbm,) * 4 + (smem,),
        scratch_shapes=[dma((4,))],
        compiler_params=pltpu.CompilerParams(vmem_limit_bytes=56 * 1024 * 1024),
        name="keep",
    )(*(pltpu.with_memory_space_constraint(x, vm) for x in outs))
    return new_factors[None], end_factor[None], new_loadings.T, end_loading.T, energy


def solution(mesh):
    torus = Mesh(mesh.devices.reshape(8, 2, 4, 2, 2), SITE + SP)
    placed = (
        P(SITE, None, SP),
        P(SITE, None, None),
        P(SP, None),
        P(SITE, None, None),
        P(SP, None),
        P(),
        P(),
        P(),
    )
    return jax.shard_map(
        local,
        mesh=torus,
        in_specs=placed,
        out_specs=(P(SITE, None, None), P(SITE, None, None), P(SP, None), P(SP, None), P()),
        check_vma=False,
    )
```
